512 devices in a mesh: tensor: 16 (over z_hi, x, core), dp: 8 (over y), tenant: 4 (over z_lo).
Axes of the slice: x: 4, y: 8, z: 8 (z_hi: 2, z_lo: 4; z = z_hi * 4 + z_lo), core: 2. Of those that a mesh axis runs over, the one named last changes fastest.
Arguments:
- output_gradient: bfloat16 [32, 384, 8192], P(('dp', 'tenant'), 'tensor'), may hold values from -6 to 6
- inputs: bfloat16 [32, 384, 8192], P(('dp', 'tenant'), None, 'tensor'), may hold values from -6 to 6
- weight: bfloat16 [8192, 8192], P('tensor', ('dp', 'tenant')), may hold values from -0.0625 to 0.0625
- adapter_down_weight: bfloat16 [128, 16, 8192], P('tenant', None, 'tensor'), may hold values from -1.5 to 1.5
- adapter_up_weight: bfloat16 [128, 16, 8192], P('tenant', None, 'tensor'), may hold values from -0.0625 to 0.0625
- block_tenant_index: int32 [32, 3], P(('dp', 'tenant')), may hold values from 0 to 31
- block_live_count: int32 [32, 3], P(('dp', 'tenant')), may hold values from 1 to 128
Outputs:
- input_gradient: bfloat16 [32, 384, 8192], P(('dp', 'tenant'), None, 'tensor')
- grad_down: float32 [128, 16, 8192], P('tenant', 'dp', 'tensor')
- grad_up: float32 [128, 16, 8192], P('tenant', 'dp', 'tensor')
The draws below stay inside these ranges and needn't reach their ends.
All inputs are finite; a program needn't handle non-finite values.
Results may differ from the reference program's by a relative error of at most 0.0065.
Values may be sent and summed in bfloat16 or wider, within the bound.
No kernel may reach another device: no remote copies, remote signals or barrier semaphores. Data moves between devices by JAX's collectives and lax.ppermute only.
A program may use at most 64 MiB of HBM per device.

```python
import jax
import jax.numpy as jnp

MODEL_WIDTH = 8192
TENANT_COUNT = 128
ADAPTER_RANK = 16
BLOCK = 128
ROWS_DEV = 384
TEN_DEV = 32
GROUPS = 32
N_DP = 8
N_TENANT = 4


def plant(array, rng, low, top_value):
    shape = array.shape
    spot = [jax.random.randint(jax.random.fold_in(rng, axis), (), 0, shape[axis]) for axis in range(len(shape))]
    array = array.at[tuple(spot)].set(low)
    longest = shape.index(max(shape))
    spot[longest] = (spot[longest] + 1) % shape[longest]
    return array.at[tuple(spot)].set(top_value)


def level_of(key, shape, shards, least, top_value):
    loudness, own = 1.0, jax.random.fold_in(key, 6)
    for axis_at, blocks in shards:
        draws = jnp.exp(jax.random.uniform(jax.random.fold_in(own, axis_at), (blocks,), jnp.float32, least / len(shards), top_value / len(shards)))
        loudness = loudness * jnp.repeat(draws, shape[axis_at] // blocks).reshape([-1 if axis == axis_at else 1 for axis in range(len(shape))])
    return loudness


def gaussian(key, extent, scale, reach, shards=(), held_as=jnp.bfloat16):
    gain = level_of(key, extent, shards, -0.22, 0.18) if shards else 1.0
    values = jax.random.normal(key, extent, jnp.float32) * scale * gain
    return jnp.minimum(jnp.maximum(values, -reach), reach).astype(held_as)


def setup_inputs(seed: int = 0) -> dict:
    seeds = jax.random.split(jax.random.key(seed), 8)
    return {
        "output_gradient": gaussian(seeds[0], (GROUPS, ROWS_DEV, MODEL_WIDTH), 1.0, 6.0, ((0, 32), (1, 16))),
        "inputs": gaussian(seeds[1], (GROUPS, ROWS_DEV, MODEL_WIDTH), 1.0, 6.0, ((0, 32), (2, 16))),
        "weight": gaussian(seeds[2], (MODEL_WIDTH, MODEL_WIDTH), MODEL_WIDTH ** -0.5, 0.0625, ((0, 16), (1, 32))),
        "adapter_down_weight": gaussian(seeds[3], (TENANT_COUNT, ADAPTER_RANK, MODEL_WIDTH), ADAPTER_RANK ** -0.5, 1.5, ((0, 4), (2, 16))),
        "adapter_up_weight": gaussian(seeds[4], (TENANT_COUNT, ADAPTER_RANK, MODEL_WIDTH), MODEL_WIDTH ** -0.5, 0.0625, ((0, 4), (2, 16))),
        "block_tenant_index": plant(jax.random.randint(seeds[5], (GROUPS, ROWS_DEV // BLOCK), 0, TEN_DEV), jax.random.fold_in(seeds[5], 1), 0, TEN_DEV - 1).astype(jnp.int32),
        "block_live_count": plant(jax.random.randint(seeds[6], (GROUPS, ROWS_DEV // BLOCK), 1, BLOCK + 1), jax.random.fold_in(seeds[6], 1), 1, BLOCK).astype(jnp.int32),
    }


adapter_scale = 2.0


def reference(output_gradient, inputs, weight, adapter_down_weight, adapter_up_weight, block_tenant_index, block_live_count):
    groups = N_DP * N_TENANT
    block_count = ROWS_DEV // BLOCK
    live_rows = jnp.arange(BLOCK, dtype=jnp.int32)[None, None, :] < block_live_count[:, :, None]
    live_rows = live_rows.reshape(groups, ROWS_DEV)
    masked = jnp.where(live_rows[:, :, None], output_gradient, jnp.zeros((), jnp.bfloat16)).astype(jnp.bfloat16)
    frozen_base_weight = jnp.dot(masked.reshape(groups * ROWS_DEV, MODEL_WIDTH), weight.T, preferred_element_type=jnp.float32)
    frozen_base_weight = frozen_base_weight.reshape(groups, block_count, BLOCK, MODEL_WIDTH)
    group_tenant_index = (jnp.arange(groups, dtype=jnp.int32) % N_TENANT)[:, None] * TEN_DEV + block_tenant_index
    group_tenant_index = group_tenant_index.astype(jnp.int32)
    selected_down_weight = adapter_down_weight[group_tenant_index].astype(jnp.float32)
    selected_up_weight = adapter_up_weight[group_tenant_index].astype(jnp.float32)
    input_block_rows = inputs.reshape(groups, block_count, BLOCK, MODEL_WIDTH).astype(jnp.float32)
    gradient_block_rows = masked.reshape(groups, block_count, BLOCK, MODEL_WIDTH).astype(jnp.float32)
    projection_input = jnp.einsum("gbmd,gbrd->gbmr", input_block_rows, selected_down_weight).astype(jnp.bfloat16).astype(jnp.float32)
    projection_output = jnp.einsum("gbmd,gbrd->gbmr", gradient_block_rows, selected_up_weight).astype(jnp.bfloat16).astype(jnp.float32)
    input_gradient = frozen_base_weight + adapter_scale * jnp.einsum("pnok,pnkv->pnov", projection_output, selected_down_weight)
    input_gradient = input_gradient.reshape(groups, ROWS_DEV, MODEL_WIDTH).astype(jnp.bfloat16)
    down_partial_products = adapter_scale * jnp.einsum("pwvq,pwva->pwqa", projection_output, input_block_rows)
    up_partial_products = adapter_scale * jnp.einsum("pwvq,pwva->pwqa", projection_input, gradient_block_rows)
    flat_index = group_tenant_index.reshape(-1)
    grad_down = jnp.zeros((TENANT_COUNT, ADAPTER_RANK, MODEL_WIDTH), jnp.float32).at[flat_index].add(down_partial_products.reshape(-1, ADAPTER_RANK, MODEL_WIDTH))
    grad_up = jnp.zeros((TENANT_COUNT, ADAPTER_RANK, MODEL_WIDTH), jnp.float32).at[flat_index].add(up_partial_products.reshape(-1, ADAPTER_RANK, MODEL_WIDTH))
    return input_gradient, grad_down, grad_up
```

```python
import jax
import jax.numpy as jnp
from jax import lax
from jax.sharding import Mesh, PartitionSpec as P

SCALE = 2.0
ZH, X, CORE, DP, TEN = 2, 4, 2, 8, 4
F32, BF16 = jnp.float32, jnp.bfloat16
TENSOR = ("zh", "x", "core")


def swap_pairs(n, bit):
    return [(i, i ^ bit) for i in range(n)]


def shift_pairs(n, offset):
    return [(i, (i + offset) % n) for i in range(n)]


def per_device(dy, inputs, weight, down, up, tenant_index, live_count):
    dy = dy[0]
    inputs = inputs[0]
    rows_here, width = dy.shape
    nrows, in_width = inputs.shape
    nblocks = live_count.shape[1]
    block = nrows // nblocks
    tenants, rank, _ = down.shape
    zh, x, core = lax.axis_index("zh"), lax.axis_index("x"), lax.axis_index("core")
    k = lax.axis_index("tenant")
    t = (zh * X + x) * CORE + core

    w_own = lax.all_gather(weight, "dp", axis=1, tiled=True)

    row = t * rows_here + lax.broadcasted_iota(jnp.int32, (rows_here, 1), 0)
    live = jnp.zeros((rows_here, 1), jnp.bool_)
    for b in range(nblocks):
        live |= (row >= b * block) & (row < b * block + live_count[0, b])
    dy = jnp.where(live, dy, jnp.zeros((), BF16))

    chunk = width // (DP * TEN)
    sets = dy.reshape(rows_here, DP, TEN, chunk).transpose(2, 0, 1, 3).reshape(TEN, rows_here, DP * chunk)
    sets = jnp.concatenate([sets, sets], axis=0)
    mine = lax.all_to_all(sets, ("zh", "tenant"), split_axis=0, concat_axis=0, tiled=True)
    group_rows = lax.all_gather(mine, "x", axis=0, tiled=False)

    hot = tenant_index[0][:, None] == lax.broadcasted_iota(jnp.int32, (nblocks, tenants), 1)
    hot = hot.astype(BF16)
    sel_down = jnp.einsum("bt,trd->brd", hot, down, preferred_element_type=F32).astype(BF16)
    sel_up = jnp.einsum("bt,trd->brd", hot, up, preferred_element_type=F32).astype(BF16)
    cols = lax.all_to_all(dy, TENSOR, split_axis=1, concat_axis=0, tiled=True)
    cols = cols.reshape(nblocks, block, -1)
    in_rows = inputs.reshape(nblocks, block, in_width)
    part_in = jnp.einsum("brd,bmd->brm", sel_down, in_rows, preferred_element_type=F32)
    part_out = jnp.einsum("brd,bmd->brm", sel_up, cols, preferred_element_type=F32)
    parts = jnp.concatenate([part_in, part_out], axis=1)
    parts = parts + lax.ppermute(parts, "core", swap_pairs(CORE, 1))
    parts = parts + lax.ppermute(parts, "x", swap_pairs(X, 1))
    parts = parts + lax.ppermute(parts, "x", swap_pairs(X, 3))
    parts = parts + lax.ppermute(parts, "zh", swap_pairs(ZH, 1))
    proj = parts.astype(BF16)
    proj_in, proj_out = proj[:, :rank], proj[:, rank:]

    w_other = lax.ppermute(w_own, "core", swap_pairs(CORE, 1))
    rows2d = group_rows.reshape(-1, DP * chunk)
    dims = (((1,), (1,)), ((), ()))
    for_other = lax.dot_general(rows2d, w_other, dims, preferred_element_type=F32).astype(BF16)
    from_other = lax.ppermute(for_other, "core", swap_pairs(CORE, 1))
    own = lax.dot_general(rows2d, w_own, dims, preferred_element_type=F32).astype(BF16)
    both = jnp.stack([own, from_other]).reshape(2, X, ZH, TEN, rows_here, in_width)

    def piece(offset):
        return lax.dynamic_index_in_dim(both, (k + offset) % TEN, 3, keepdims=False)

    total = piece(0).astype(F32)
    for offset in (2, 1, 3):
        total = total + lax.ppermute(piece(offset), "tenant", shift_pairs(TEN, offset)).astype(F32)
    total = jnp.where(core == 0, total, total[::-1])
    total = total.transpose(2, 1, 0, 3, 4).reshape(nblocks, block, in_width)
    adapter = jnp.einsum("brm,brd->bmd", proj_out, sel_down, preferred_element_type=F32)
    input_gradient = (total + SCALE * adapter).astype(BF16).reshape(1, nrows, in_width)

    g_down = SCALE * jnp.einsum("brm,bmd->brd", proj_out, in_rows, preferred_element_type=F32)
    g_up = SCALE * jnp.einsum("brm,bmd->brd", proj_in, cols, preferred_element_type=F32)
    share = rank // DP
    grads = jnp.stack([g_down, g_up]).reshape(2, nblocks, DP, share, in_width).transpose(2, 0, 1, 3, 4)
    grads = grads.reshape(DP, 2 * nblocks * share, in_width)
    ids = jnp.zeros((in_width,), F32)
    lane = lax.broadcasted_iota(jnp.int32, (in_width,), 0)
    for b in range(nblocks):
        ids = jnp.where(lane == b, tenant_index[0, b].astype(F32), ids)
    ids = jnp.broadcast_to(ids, (DP, 1, in_width))
    sent = jnp.concatenate([grads, ids], axis=1)
    got = lax.all_to_all(sent, "dp", split_axis=0, concat_axis=0, tiled=True)
    ids = got[:, -1, :nblocks].astype(jnp.int32)
    got = got[:, :-1].reshape(DP, 2, nblocks, share, in_width)
    place = (ids[None] == lax.broadcasted_iota(jnp.int32, (tenants, DP, nblocks), 0)).astype(F32)
    out = jnp.einsum("tgb,gabsd->atsd", place, got, precision=lax.Precision.HIGHEST, preferred_element_type=F32)
    return input_gradient, out[0], out[1]


def solution(mesh):
    fine = Mesh(mesh.devices.reshape(ZH, X, CORE, DP, TEN), ("zh", "x", "core", "dp", "tenant"))
    group = ("dp", "tenant")
    return jax.shard_map(
        per_device,
        mesh=fine,
        in_specs=(
            P(group, TENSOR, None),
            P(group, None, TENSOR),
            P(TENSOR, group),
            P("tenant", None, TENSOR),
            P("tenant", None, TENSOR),
            P(group, None),
            P(group, None),
        ),
        out_specs=(P(group, None, TENSOR), P("tenant", "dp", TENSOR), P("tenant", "dp", TENSOR)),
        check_vma=False,
    )
```

```python
import functools

import jax
import jax.numpy as jnp
from jax import lax
from jax.experimental import pallas as pl
from jax.experimental.pallas import tpu as pltpu
from jax.sharding import Mesh, PartitionSpec as P

SCALE = 2.0
ZH, X, CORE, DP, KH, KL = 2, 4, 2, 8, 2, 2
TENSOR, TENANT = ("zh", "x", "core"), ("kh", "kl")
AXES = TENSOR + ("dp",) + TENANT
F32, BF16 = jnp.float32, jnp.bfloat16
GROUPS = ((0, 1, 3), (2,))
VMEM_LIMIT = 48 * 2**20


def exchange(blocks, axes):
    return lax.all_to_all(blocks, axes, split_axis=0, concat_axis=0, tiled=True)


def swap_pairs(n, bit):
    return [(i, i ^ bit) for i in range(n)]


def shift_pairs(n, offset):
    return [(i, (i + offset) % n) for i in range(n)]


def split_kernel(nblocks, block, at_ref, live_ref, dy_ref, same_ref, other_ref, cols_ref):
    rows, width = dy_ref.shape
    first, kh, kl = at_ref[0], at_ref[1], at_ref[2]
    row = first + lax.broadcasted_iota(jnp.int32, (rows, 1), 0)
    live = jnp.zeros((rows, 1), jnp.int32)
    for b in range(nblocks):
        inside = (row >= b * block) & (row < b * block + live_ref[0, b])
        live = jnp.where(inside, 1, live)
    live = live > 0
    chunk = width // (DP * KH * KL)
    wide = cols_ref.shape[2]
    for d in range(DP):
        to = slice(d * chunk, (d + 1) * chunk)
        for low in range(KL):
            parts = []
            for h in range(KH):
                at = ((d * KH + h) * KL + low) * chunk
                part = jnp.where(live, dy_ref[:, at : at + chunk].astype(F32), 0.0)
                cols_ref[at // wide, :, at % wide : at % wide + chunk] = part.astype(BF16)
                parts.append(part)
            slot = lax.rem(kl + low, KL)
            same_ref[slot, :, to] = jnp.where(kh == 0, parts[0], parts[1]).astype(BF16)
            other_ref[slot, :, to] = jnp.where(kh == 0, parts[1], parts[0]).astype(BF16)


def split_rows(dy, at, live_count, nblocks, block):
    rows, width = dy.shape
    half = jax.ShapeDtypeStruct((KL, rows, width // (KH * KL)), BF16)
    shapes = [half, half, jax.ShapeDtypeStruct((ZH * X * CORE, rows, width // (ZH * X * CORE)), BF16)]
    vmem = pl.BlockSpec(memory_space=pltpu.VMEM)
    smem = pl.BlockSpec(memory_space=pltpu.SMEM)
    return pl.pallas_call(
        functools.partial(split_kernel, nblocks, block),
        out_shape=shapes,
        in_specs=[smem, smem, vmem],
        out_specs=[vmem] * len(shapes),
        cost_estimate=pl.CostEstimate(flops=0, bytes_accessed=3 * rows * width * 2, transcendentals=0),
        compiler_params=pltpu.CompilerParams(vmem_limit_bytes=VMEM_LIMIT),
        name="split_rows",
    )(at, live_count, dy)


def base_kernel(count, w_ref, *refs):
    pieces, keep_ref, send_ref = refs[:count], refs[count], refs[count + 1]
    m = pieces[0].shape[2]
    feats, chunk = w_ref.shape[2:]
    total = None
    for h in range(KL):
        rows = [piece[:, h].reshape(KH * ZH * m, DP * chunk) for piece in pieces]
        rows = jnp.concatenate(rows, axis=0)
        for d in range(DP):
            term = lax.dot_general(
                rows[:, d * chunk : (d + 1) * chunk], w_ref[d, h], (((1,), (1,)), ((), ())), preferred_element_type=F32
            )
            total = term if total is None else total + term
    total = total.reshape(count, KH, ZH, m, feats)
    keep_ref[...] = total[:, 0].reshape(keep_ref.shape)
    send_ref[...] = total[:, 1].reshape(send_ref.shape).astype(BF16)


def base_product(weights, pieces):
    count, m, feats = len(pieces), pieces[0].shape[2], weights.shape[2]
    vmem = pl.BlockSpec(memory_space=pltpu.VMEM)
    rows = count * ZH * KH * m
    shape = (count * ZH, m, feats)
    return pl.pallas_call(
        functools.partial(base_kernel, count),
        out_shape=[jax.ShapeDtypeStruct(shape, F32), jax.ShapeDtypeStruct(shape, BF16)],
        in_specs=[vmem] * (1 + count),
        out_specs=[vmem] * 2,
        cost_estimate=pl.CostEstimate(
            flops=2 * rows * weights.size, bytes_accessed=2 * (count * pieces[0].size + weights.size + rows * feats), transcendentals=0
        ),
        compiler_params=pltpu.CompilerParams(vmem_limit_bytes=VMEM_LIMIT),
        name="base_product",
    )(weights, *pieces)


def parts_kernel(down_ref, up_ref, in_ref, cols_ref, out_ref):
    nblocks = down_ref.shape[0]
    block = in_ref.shape[0] // nblocks
    dims = (((1,), (1,)), ((), ()))
    for i, (factor, rows_ref) in enumerate(((down_ref, in_ref), (up_ref, cols_ref))):
        for b in range(nblocks):
            rows = rows_ref[b * block : (b + 1) * block, :]
            part = lax.dot_general(factor[b], rows, dims, preferred_element_type=F32)
            for to in range(out_ref.shape[0]):
                out_ref[to, i * nblocks + b] = part


def rank_parts(sel_down, sel_up, inputs, cols):
    nblocks, rank, _ = sel_down.shape
    vmem = pl.BlockSpec(memory_space=pltpu.VMEM)
    return pl.pallas_call(
        parts_kernel,
        out_shape=jax.ShapeDtypeStruct((X * CORE, 2 * nblocks, rank, inputs.shape[0] // nblocks), F32),
        in_specs=[vmem] * 4,
        out_specs=vmem,
        cost_estimate=pl.CostEstimate(flops=4 * rank * inputs.size, bytes_accessed=6 * inputs.size, transcendentals=0),
        compiler_params=pltpu.CompilerParams(vmem_limit_bytes=VMEM_LIMIT),
        name="rank_parts",
    )(sel_down, sel_up, inputs, cols)


def grads_kernel(ids_ref, own_ref, got_ref, in_ref, cols_ref, out_ref, proj_ref):
    nblocks = own_ref.shape[0] // 2
    block, wide = in_ref.shape[0] // nblocks, in_ref.shape[1]
    share = own_ref.shape[1] // DP
    proj = (own_ref[...] + got_ref[...]).astype(BF16)
    proj_ref[...] = proj[nblocks:]
    dims = (((1,), (0,)), ((), ()))
    for b in range(nblocks):
        rows = slice(b * block, (b + 1) * block)
        down = lax.dot_general(proj[nblocks + b], in_ref[rows, :], dims, preferred_element_type=F32)
        up = lax.dot_general(proj[b], cols_ref[rows, :], dims, preferred_element_type=F32)
        for i, grad in enumerate((SCALE * down, SCALE * up)):
            at = (i * nblocks + b) * share
            for to in range(DP):
                out_ref[to, at : at + share, :] = grad[to * share : (to + 1) * share]
    lane = lax.broadcasted_iota(jnp.int32, (1, wide), 1)
    ids = jnp.zeros((1, wide), F32)
    for b in range(nblocks):
        ids = jnp.where(lane == b, ids_ref[0, b].astype(F32), ids)
    for to in range(DP):
        out_ref[to, 2 * nblocks * share :, :] = ids


def block_grads(tenant_index, own, got, inputs, cols):
    count, rank, block = own.shape
    nblocks = count // 2
    wide = inputs.shape[1]
    vmem = pl.BlockSpec(memory_space=pltpu.VMEM)
    smem = pl.BlockSpec(memory_space=pltpu.SMEM)
    return pl.pallas_call(
        grads_kernel,
        out_shape=[
            jax.ShapeDtypeStruct((DP, 2 * nblocks * rank // DP + 1, wide), F32),
            jax.ShapeDtypeStruct((nblocks, rank, block), BF16),
        ],
        in_specs=[smem] + [vmem] * 4,
        out_specs=[vmem, vmem],
        cost_estimate=pl.CostEstimate(flops=4 * rank * inputs.size, bytes_accessed=6 * inputs.size, transcendentals=0),
        compiler_params=pltpu.CompilerParams(vmem_limit_bytes=VMEM_LIMIT),
        name="block_grads",
    )(tenant_index, own, got, inputs, cols)


def join_kernel(nblocks, group_sizes, where_ref, proj_ref, down_ref, *refs):
    adapter_ref, out_ref = refs[-1], refs[-2]
    m = out_ref.shape[1]
    terms = [
        SCALE
        * lax.dot_general(proj_ref[b], down_ref[b], (((0,), (0,)), ((), ())), preferred_element_type=F32)
        for b in range(nblocks)
    ]
    adapter_ref[...] = jnp.concatenate(terms, axis=0).reshape(adapter_ref.shape)
    at, place = 0, 0
    for size in group_sizes:
        keep, got = refs[at : at + 2]
        at += 2
        for p in range(size):
            for z in range(ZH):
                to = where_ref[place]
                place += 1
                total = keep[p * ZH + z] + got[p * ZH + z].astype(F32) + adapter_ref[to]
                out_ref[to] = total.astype(BF16)


def join(where, proj_out, sel_down, groups):
    m, feats = groups[0][0].shape[1:]
    blocks = ZH * X * CORE
    vmem = pl.BlockSpec(memory_space=pltpu.VMEM)
    smem = pl.BlockSpec(memory_space=pltpu.SMEM)
    parts = [part for group in groups for part in group]
    return pl.pallas_call(
        functools.partial(join_kernel, proj_out.shape[0], [group[0].shape[0] // ZH for group in groups]),
        out_shape=jax.ShapeDtypeStruct((blocks, m, feats), BF16),
        in_specs=[smem] + [vmem] * (2 + len(parts)),
        out_specs=vmem,
        scratch_shapes=[pltpu.VMEM((blocks, m, feats), F32)],
        cost_estimate=pl.CostEstimate(flops=0, bytes_accessed=10 * blocks * m * feats, transcendentals=0),
        compiler_params=pltpu.CompilerParams(vmem_limit_bytes=VMEM_LIMIT),
        name="join_rows",
    )(where, proj_out, sel_down, *parts)


def per_device(dy, inputs, weight, down, up, tenant_index, live_count):
    dy, inputs = dy[0], inputs[0]
    rows_here = dy.shape[0]
    nrows, in_width = inputs.shape
    nblocks = live_count.shape[1]
    block = nrows // nblocks
    tenants, rank, _ = down.shape
    zh, x, core = lax.axis_index("zh"), lax.axis_index("x"), lax.axis_index("core")
    kh, kl = lax.axis_index("kh"), lax.axis_index("kl")
    t = (zh * X + x) * CORE + core

    at = jnp.stack([t * rows_here, kh, kl]).astype(jnp.int32)
    same, other, cols = split_rows(dy, at, live_count, nblocks, block)

    swapped, _ = lax.optimization_barrier((lax.ppermute(weight, "kl", swap_pairs(KL, 1)), same))
    weights = lax.all_gather(jnp.stack([weight, swapped]), "dp", axis=0, tiled=False)

    from_zh = lax.ppermute(same, "zh", swap_pairs(ZH, 1))
    from_both = lax.ppermute(other, ("zh", "kh"), swap_pairs(ZH * KH, 3))
    from_kh = lax.ppermute(other, "kh", swap_pairs(KH, 1))
    mine = jnp.stack([same, from_zh, from_kh, from_both])
    hot = tenant_index[0][:, None] == lax.broadcasted_iota(jnp.int32, (nblocks, tenants), 1)
    hot = hot.astype(BF16)
    sel_down = jnp.einsum("bt,trd->brd", hot, down, preferred_element_type=F32).astype(BF16)
    sel_up = jnp.einsum("bt,trd->brd", hot, up, preferred_element_type=F32).astype(BF16)
    cols = exchange(cols, TENSOR).reshape(nrows, -1)
    parts = exchange(rank_parts(sel_down, sel_up, inputs, cols), ("x", "core"))
    parts, mine = lax.optimization_barrier((parts, mine))
    parts = parts.sum(axis=0)
    parts_got = lax.ppermute(parts, "zh", swap_pairs(ZH, 1))

    share = rank // DP
    grads, proj_out = block_grads(tenant_index, parts, parts_got, inputs, cols)
    got = exchange(grads, "dp")

    from_x = {0: mine}
    for offset in (1, 3, 2):
        from_x[offset] = lax.ppermute(mine, "x", shift_pairs(X, offset))
    for offset in (1, 3):
        from_x[offset], got = lax.optimization_barrier((from_x[offset], got))
    groups, where, swapped = [], [], []
    for offsets in GROUPS:
        pieces = []
        for offset in offsets:
            swapped.append(lax.ppermute(from_x[offset], "core", swap_pairs(CORE, 1)))
            pieces += [from_x[offset], swapped[-1]]
            for c in (core, 1 - core):
                where += [((zh + z) % ZH * X + (x + X - offset) % X) * CORE + c for z in range(ZH)]
        keep, send = base_product(weights, pieces)
        groups.append([keep, lax.ppermute(send, "kh", swap_pairs(KH, 1))])
    where = jnp.stack(where).astype(jnp.int32)

    ids = got[:, -1, :nblocks].astype(jnp.int32)
    got = got[:, :-1].reshape(DP, 2, nblocks, share, in_width)
    place = (ids[None] == lax.broadcasted_iota(jnp.int32, (tenants, DP, nblocks), 0)).astype(F32)
    out = jnp.einsum("tgb,gabsd->atsd", place, got, precision=lax.Precision.HIGHEST, preferred_element_type=F32)

    input_gradient = join(where, proj_out, sel_down, groups).reshape(1, nrows, in_width)
    return input_gradient, out[0], out[1]


def solution(mesh):
    fine = Mesh(mesh.devices.reshape(ZH, X, CORE, DP, KH, KL), AXES)
    group = ("dp",) + TENANT
    return jax.shard_map(
        per_device,
        mesh=fine,
        in_specs=(
            P(group, TENSOR, None),
            P(group, None, TENSOR),
            P(TENSOR, group),
            P(TENANT, None, TENSOR),
            P(TENANT, None, TENSOR),
            P(group, None),
            P(group, None),
        ),
        out_specs=(P(group, None, TENSOR), P(TENANT, "dp", TENSOR), P(TENANT, "dp", TENSOR)),
        check_vma=False,
    )
```

```python
import functools

import jax
import jax.numpy as jnp
from jax import lax
from jax.experimental import pallas as pl
from jax.experimental.pallas import tpu as pltpu
from jax.sharding import Mesh, PartitionSpec as P

SCALE = 2.0
ZH, X, CORE, DP, KH, KL = 2, 4, 2, 8, 2, 2
TENSOR, TENANT = ("zh", "x", "core"), ("kh", "kl")
AXES = TENSOR + ("dp",) + TENANT
F32, BF16 = jnp.float32, jnp.bfloat16
OFFSETS = (0, 1, 3, 2)
VMEM_LIMIT = 12 * 2**20


def exchange(blocks, axes):
    return lax.all_to_all(blocks, axes, split_axis=0, concat_axis=0, tiled=True)


def swap_pairs(n, bit):
    return [(i, i ^ bit) for i in range(n)]


def shift_pairs(n, offset):
    return [(i, (i + offset) % n) for i in range(n)]


def split_kernel(nblocks, block, at_ref, live_ref, dy_ref, same_ref, other_ref, cols_ref):
    rows, width = dy_ref.shape
    first, kh, kl = at_ref[0], at_ref[1], at_ref[2]
    row = first + lax.broadcasted_iota(jnp.int32, (rows, 1), 0)
    live = jnp.zeros((rows, 1), jnp.int32)
    for b in range(nblocks):
        inside = (row >= b * block) & (row < b * block + live_ref[0, b])
        live = jnp.where(inside, 1, live)
    live = live > 0
    chunk = width // (DP * KH * KL)
    wide = cols_ref.shape[2]
    for d in range(DP):
        to = slice(d * chunk, (d + 1) * chunk)
        for low in range(KL):
            parts = []
            for h in range(KH):
                at = ((d * KH + h) * KL + low) * chunk
                part = jnp.where(live, dy_ref[:, at : at + chunk].astype(F32), 0.0)
                cols_ref[at // wide, :, at % wide : at % wide + chunk] = part.astype(BF16)
                parts.append(part)
            slot = lax.rem(kl + low, KL)
            same_ref[slot, :, to] = jnp.where(kh == 0, parts[0], parts[1]).astype(BF16)
            other_ref[slot, :, to] = jnp.where(kh == 0, parts[1], parts[0]).astype(BF16)


def split_rows(dy, at, live_count, nblocks, block):
    rows, width = dy.shape
    half = jax.ShapeDtypeStruct((KL, rows, width // (KH * KL)), BF16)
    shapes = [half, half, jax.ShapeDtypeStruct((ZH * X * CORE, rows, width // (ZH * X * CORE)), BF16)]
    vmem = pl.BlockSpec(memory_space=pltpu.VMEM)
    smem = pl.BlockSpec(memory_space=pltpu.SMEM)
    return pl.pallas_call(
        functools.partial(split_kernel, nblocks, block),
        out_shape=shapes,
        in_specs=[smem, smem, vmem],
        out_specs=[vmem] * len(shapes),
        cost_estimate=pl.CostEstimate(flops=0, bytes_accessed=3 * rows * width * 2, transcendentals=0),
        compiler_params=pltpu.CompilerParams(vmem_limit_bytes=VMEM_LIMIT),
        name="split_rows",
    )(at, live_count, dy)


def base_kernel(core_ref, w_ref, *refs):
    pieces, outs = refs[:-CORE], refs[-CORE:]
    zs, _, m, depth = pieces[0].shape
    chunk = w_ref.shape[3]
    for h in range(KL):
        rows = jnp.concatenate([piece[:, h].reshape(zs * m, depth) for piece in pieces], axis=0)
        if h == 0:
            first = rows
    for i, out in enumerate(outs):
        at = lax.rem(core_ref[0] + i, CORE)
        total = None
        for h, rows_h in enumerate((first, rows)):
            for d in range(DP):
                term = lax.dot_general(
                    rows_h[:, d * chunk : (d + 1) * chunk], w_ref[d, at, h], (((1,), (0,)), ((), ())), preferred_element_type=F32
                )
                total = term if total is None else total + term
        out[...] = total.reshape(out.shape).astype(out.dtype)


def base_product(core, weights, pieces, dtypes):
    zs, _, m, _ = pieces[0].shape
    count, feats = len(pieces) * zs, weights.shape[4]
    vmem = pl.BlockSpec(memory_space=pltpu.VMEM)
    smem = pl.BlockSpec(memory_space=pltpu.SMEM)
    return pl.pallas_call(
        base_kernel,
        out_shape=[jax.ShapeDtypeStruct((count, m, feats), dtype) for dtype in dtypes],
        in_specs=[smem, vmem] + [vmem] * len(pieces),
        out_specs=[vmem] * CORE,
        cost_estimate=pl.CostEstimate(
            flops=2 * count * m * weights.size,
            bytes_accessed=2 * (len(pieces) * pieces[0].size + weights.size + 2 * count * m * feats),
            transcendentals=0,
        ),
        compiler_params=pltpu.CompilerParams(vmem_limit_bytes=2 * VMEM_LIMIT),
        name="base_product",
    )(core, weights, *pieces)


def parts_kernel(down_ref, up_ref, in_ref, cols_ref, out_ref):
    nblocks = down_ref.shape[0]
    block = in_ref.shape[0] // nblocks
    dims = (((1,), (1,)), ((), ()))
    for i, (factor, rows_ref) in enumerate(((down_ref, in_ref), (up_ref, cols_ref))):
        for b in range(nblocks):
            rows = rows_ref[b * block : (b + 1) * block, :]
            part = lax.dot_general(factor[b], rows, dims, preferred_element_type=F32)
            for to in range(out_ref.shape[0]):
                out_ref[to, i * nblocks + b] = part


def rank_parts(sel_down, sel_up, inputs, cols):
    nblocks, rank, _ = sel_down.shape
    vmem = pl.BlockSpec(memory_space=pltpu.VMEM)
    return pl.pallas_call(
        parts_kernel,
        out_shape=jax.ShapeDtypeStruct((X * CORE, 2 * nblocks, rank, inputs.shape[0] // nblocks), F32),
        in_specs=[vmem] * 4,
        out_specs=vmem,
        cost_estimate=pl.CostEstimate(flops=4 * rank * inputs.size, bytes_accessed=6 * inputs.size, transcendentals=0),
        compiler_params=pltpu.CompilerParams(vmem_limit_bytes=VMEM_LIMIT),
        name="rank_parts",
    )(sel_down, sel_up, inputs, cols)


def grads_kernel(ids_ref, own_ref, got_ref, in_ref, cols_ref, out_ref, proj_ref):
    nblocks = own_ref.shape[0] // 2
    block, wide = in_ref.shape[0] // nblocks, in_ref.shape[1]
    share = own_ref.shape[1] // DP
    proj = (own_ref[...] + got_ref[...]).astype(BF16)
    proj_ref[...] = proj[nblocks:]
    dims = (((1,), (0,)), ((), ()))
    for b in range(nblocks):
        rows = slice(b * block, (b + 1) * block)
        down = lax.dot_general(proj[nblocks + b], in_ref[rows, :], dims, preferred_element_type=F32)
        up = lax.dot_general(proj[b], cols_ref[rows, :], dims, preferred_element_type=F32)
        for i, grad in enumerate((SCALE * down, SCALE * up)):
            at = (i * nblocks + b) * share
            for to in range(DP):
                out_ref[to, at : at + share, :] = grad[to * share : (to + 1) * share]
    lane = lax.broadcasted_iota(jnp.int32, (1, wide), 1)
    ids = jnp.zeros((1, wide), F32)
    for b in range(nblocks):
        ids = jnp.where(lane == b, ids_ref[0, b].astype(F32), ids)
    for to in range(DP):
        out_ref[to, 2 * nblocks * share :, :] = ids


def block_grads(tenant_index, own, got, inputs, cols):
    count, rank, block = own.shape
    nblocks = count // 2
    wide = inputs.shape[1]
    vmem = pl.BlockSpec(memory_space=pltpu.VMEM)
    smem = pl.BlockSpec(memory_space=pltpu.SMEM)
    return pl.pallas_call(
        grads_kernel,
        out_shape=[
            jax.ShapeDtypeStruct((DP, 2 * nblocks * rank // DP + 1, wide), F32),
            jax.ShapeDtypeStruct((nblocks, rank, block), BF16),
        ],
        in_specs=[smem] + [vmem] * 4,
        out_specs=[vmem, vmem],
        cost_estimate=pl.CostEstimate(flops=4 * rank * inputs.size, bytes_accessed=6 * inputs.size, transcendentals=0),
        compiler_params=pltpu.CompilerParams(vmem_limit_bytes=VMEM_LIMIT),
        name="block_grads",
    )(tenant_index, own, got, inputs, cols)


def join_kernel(nblocks, where_ref, proj_ref, down_ref, *refs):
    *parts, out_ref, adapter_ref = refs
    dims = (((0,), (0,)), ((), ()))
    terms = [SCALE * lax.dot_general(proj_ref[b], down_ref[b], dims, preferred_element_type=F32) for b in range(nblocks)]
    adapter_ref[...] = jnp.concatenate(terms, axis=0).reshape(adapter_ref.shape)
    for c in range(CORE):
        keep, got = parts[2 * c : 2 * c + 2]
        for p in range(keep.shape[0]):
            to = where_ref[c * keep.shape[0] + p]
            out_ref[to] = (keep[p].astype(F32) + got[p].astype(F32) + adapter_ref[to]).astype(BF16)


def join(where, proj_out, sel_down, parts):
    count, m, feats = parts[0].shape
    shape = (CORE * count, m, feats)
    vmem = pl.BlockSpec(memory_space=pltpu.VMEM)
    smem = pl.BlockSpec(memory_space=pltpu.SMEM)
    return pl.pallas_call(
        functools.partial(join_kernel, proj_out.shape[0]),
        out_shape=jax.ShapeDtypeStruct(shape, BF16),
        in_specs=[smem] + [vmem] * (2 + len(parts)),
        out_specs=vmem,
        scratch_shapes=[pltpu.VMEM(shape, F32)],
        cost_estimate=pl.CostEstimate(flops=0, bytes_accessed=20 * count * m * feats, transcendentals=0),
        compiler_params=pltpu.CompilerParams(vmem_limit_bytes=VMEM_LIMIT),
        name="join_rows",
    )(where, proj_out, sel_down, *parts)


def per_device(dy, inputs, weight, down, up, tenant_index, live_count):
    dy, inputs = dy[0], inputs[0]
    rows_here = dy.shape[0]
    nrows, in_width = inputs.shape
    nblocks = live_count.shape[1]
    block = nrows // nblocks
    tenants, rank, _ = down.shape
    zh, x, core = lax.axis_index("zh"), lax.axis_index("x"), lax.axis_index("core")
    kh, kl = lax.axis_index("kh"), lax.axis_index("kl")
    t = (zh * X + x) * CORE + core

    at = jnp.stack([t * rows_here, kh, kl]).astype(jnp.int32)
    same, other, cols = split_rows(dy, at, live_count, nblocks, block)

    swapped, _ = lax.optimization_barrier((lax.ppermute(weight, "kl", swap_pairs(KL, 1)), same))
    weights = lax.all_gather(jnp.stack([weight.T, swapped.T]), ("dp", "core"), axis=0, tiled=False)
    weights = weights.reshape((DP, CORE, KL) + weight.T.shape)

    from_zh = lax.ppermute(same, "zh", swap_pairs(ZH, 1))
    from_both = lax.ppermute(other, ("zh", "kh"), swap_pairs(ZH * KH, 3))
    from_kh = lax.ppermute(other, "kh", swap_pairs(KH, 1))
    away, home = jnp.stack([from_kh, from_both]), jnp.stack([same, from_zh])
    hot = tenant_index[0][:, None] == lax.broadcasted_iota(jnp.int32, (nblocks, tenants), 1)
    hot = hot.astype(BF16)
    sel_down = jnp.einsum("bt,trd->brd", hot, down, preferred_element_type=F32).astype(BF16)
    sel_up = jnp.einsum("bt,trd->brd", hot, up, preferred_element_type=F32).astype(BF16)
    cols = exchange(cols, TENSOR)
    cols = cols.reshape(nrows, -1)
    parts = rank_parts(sel_down, sel_up, inputs, cols)
    parts = exchange(parts, ("x", "core"))
    parts, away, home = lax.optimization_barrier((parts, away, home))
    parts = parts.sum(axis=0)
    parts_got = lax.ppermute(parts, "zh", swap_pairs(ZH, 1))

    share = rank // DP
    grads, proj_out = block_grads(tenant_index, parts, parts_got, inputs, cols)

    away = [lax.ppermute(away, "x", shift_pairs(X, offset)) if offset else away for offset in OFFSETS]
    home = [lax.ppermute(home, "x", shift_pairs(X, offset)) if offset else home for offset in OFFSETS]
    away, grads = lax.optimization_barrier((away, grads))
    core_at = core[None].astype(jnp.int32)
    send, send_other = base_product(core_at, weights, away, (BF16, BF16))
    sums = lax.ppermute(send, "kh", swap_pairs(KH, 1))
    sums_other = lax.ppermute(send_other, ("core", "kh"), swap_pairs(CORE * KH, 3))
    grads, send = lax.optimization_barrier((grads, send))
    got = exchange(grads, "dp")
    home, send, got = lax.optimization_barrier((home, send, got))
    keep, keep_other = base_product(core_at, weights, home, (F32, BF16))
    keep_other = lax.ppermute(keep_other, "core", swap_pairs(CORE, 1))
    where = [
        ((zh + z) % ZH * X + (x + X - offset) % X) * CORE + c
        for c in (core, 1 - core) for offset in OFFSETS for z in range(ZH)
    ]
    where = jnp.stack(where).astype(jnp.int32)

    ids = got[:, -1, :nblocks].astype(jnp.int32)
    got = got[:, :-1].reshape(DP, 2, nblocks, share, in_width)
    place = (ids[None] == lax.broadcasted_iota(jnp.int32, (tenants, DP, nblocks), 0)).astype(F32)
    out = jnp.einsum("tgb,gabsd->atsd", place, got, precision=lax.Precision.HIGHEST, preferred_element_type=F32)

    input_gradient = join(where, proj_out, sel_down, (keep, sums, keep_other, sums_other)).reshape(1, nrows, in_width)
    return input_gradient, out[0], out[1]


def solution(mesh):
    fine = Mesh(mesh.devices.reshape(ZH, X, CORE, DP, KH, KL), AXES)
    group = ("dp",) + TENANT
    return jax.shard_map(
        per_device,
        mesh=fine,
        in_specs=(
            P(group, TENSOR, None),
            P(group, None, TENSOR),
            P(TENSOR, group),
            P(TENANT, None, TENSOR),
            P(TENANT, None, TENSOR),
            P(group, None),
            P(group, None),
        ),
        out_specs=(P(group, None, TENSOR), P(TENANT, "dp", TENSOR), P(TENANT, "dp", TENSOR)),
        check_vma=False,
    )
```

```python
import functools

import jax
import jax.numpy as jnp
from jax import lax
from jax.experimental import pallas as pl
from jax.experimental.pallas import tpu as pltpu
from jax.sharding import Mesh, PartitionSpec as P

SCALE = 2.0
ZH, X, CORE, DP, KH, KL = 2, 4, 2, 8, 2, 2
TENSOR, TENANT = ("zh", "x", "core"), ("kh", "kl")
AXES = TENSOR + ("dp",) + TENANT
F32, BF16 = jnp.float32, jnp.bfloat16
OFFSETS = (0, 1, 3, 2)
VMEM_LIMIT = 12 * 2**20


def exchange(blocks, axes):
    return lax.all_to_all(blocks, axes, split_axis=0, concat_axis=0, tiled=True)


def swap_pairs(n, bit):
    return [(i, i ^ bit) for i in range(n)]


def shift_pairs(n, offset):
    return [(i, (i + offset) % n) for i in range(n)]


def split_kernel(nblocks, block, at_ref, live_ref, dy_ref, same_ref, other_ref, cols_ref):
    rows, width = dy_ref.shape
    first, kh, kl = at_ref[0], at_ref[1], at_ref[2]
    row = first + lax.broadcasted_iota(jnp.int32, (rows, 1), 0)
    live = jnp.zeros((rows, 1), jnp.int32)
    for b in range(nblocks):
        inside = (row >= b * block) & (row < b * block + live_ref[0, b])
        live = jnp.where(inside, 1, live)
    live = live > 0
    chunk = width // (DP * KH * KL)
    wide = cols_ref.shape[2]
    for d in range(DP):
        to = slice(d * chunk, (d + 1) * chunk)
        for low in range(KL):
            parts = []
            for h in range(KH):
                at = ((d * KH + h) * KL + low) * chunk
                part = jnp.where(live, dy_ref[:, at : at + chunk].astype(F32), 0.0)
                cols_ref[at // wide, :, at % wide : at % wide + chunk] = part.astype(BF16)
                parts.append(part)
            slot = lax.rem(kl + low, KL)
            same_ref[slot, :, to] = jnp.where(kh == 0, parts[0], parts[1]).astype(BF16)
            other_ref[slot, :, to] = jnp.where(kh == 0, parts[1], parts[0]).astype(BF16)


def split_rows(dy, at, live_count, nblocks, block):
    rows, width = dy.shape
    half = jax.ShapeDtypeStruct((KL, rows, width // (KH * KL)), BF16)
    shapes = [half, half, jax.ShapeDtypeStruct((ZH * X * CORE, rows, width // (ZH * X * CORE)), BF16)]
    vmem = pl.BlockSpec(memory_space=pltpu.VMEM)
    smem = pl.BlockSpec(memory_space=pltpu.SMEM)
    return pl.pallas_call(
        functools.partial(split_kernel, nblocks, block),
        out_shape=shapes,
        in_specs=[smem, smem, vmem],
        out_specs=[vmem] * len(shapes),
        cost_estimate=pl.CostEstimate(flops=0, bytes_accessed=3 * rows * width * 2, transcendentals=0),
        compiler_params=pltpu.CompilerParams(vmem_limit_bytes=VMEM_LIMIT),
        name="split_rows",
    )(at, live_count, dy)


def turn_kernel(own_ref, got_ref, out_ref):
    out_ref[0] = own_ref[...].T
    out_ref[1] = got_ref[...].T


def turned(own, got):
    vmem = pl.BlockSpec(memory_space=pltpu.VMEM)
    return pl.pallas_call(
        turn_kernel,
        out_shape=jax.ShapeDtypeStruct((KL,) + own.shape[::-1], own.dtype),
        in_specs=[vmem, vmem],
        out_specs=vmem,
        cost_estimate=pl.CostEstimate(flops=0, bytes_accessed=8 * own.size, transcendentals=0),
        compiler_params=pltpu.CompilerParams(vmem_limit_bytes=VMEM_LIMIT),
        name="turned",
    )(own, got)


def base_kernel(core_ref, w_ref, *refs):
    pieces, outs, held_ref, sems = refs[: -CORE - 2], refs[-CORE - 2 : -2], refs[-2], refs[-1]
    copies = [pltpu.make_async_copy(w_ref.at[d], held_ref.at[d], sems.at[d]) for d in range(DP)]
    for copy in copies:
        copy.start()
    if len(pieces[0].shape) > 4:
        pieces = [pieces[0][i] for i in range(pieces[0].shape[0])]
    zs, _, m, depth = pieces[0].shape
    chunk = w_ref.shape[3]
    rows = [jnp.concatenate([piece[:, h].reshape(zs * m, depth) for piece in pieces], axis=0) for h in range(KL)]
    totals = [None] * CORE
    for d, copy in enumerate(copies):
        copy.wait()
        for i in range(CORE):
            at = lax.rem(core_ref[0] + i, CORE)
            for h in range(KL):
                term = lax.dot_general(
                    rows[h][:, d * chunk : (d + 1) * chunk], held_ref[d, at, h], (((1,), (0,)), ((), ())), preferred_element_type=F32
                )
                totals[i] = term if totals[i] is None else totals[i] + term
    for out, total in zip(outs, totals):
        out[...] = total.reshape(out.shape).astype(out.dtype)


def base_product(core, weights, pieces, dtypes):
    zs, _, m, _ = pieces[0].shape[-4:]
    count, feats = X * zs, weights.shape[4]
    vmem = pl.BlockSpec(memory_space=pltpu.VMEM)
    smem = pl.BlockSpec(memory_space=pltpu.SMEM)
    return pl.pallas_call(
        base_kernel,
        out_shape=[jax.ShapeDtypeStruct((count, m, feats), dtype) for dtype in dtypes],
        in_specs=[smem, pl.BlockSpec(memory_space=pl.ANY)] + [vmem] * len(pieces),
        out_specs=[vmem] * CORE,
        scratch_shapes=[pltpu.VMEM(weights.shape, weights.dtype), pltpu.SemaphoreType.DMA((DP,))],
        cost_estimate=pl.CostEstimate(
            flops=2 * count * m * weights.size,
            bytes_accessed=2 * (sum(p.size for p in pieces) + weights.size + 2 * count * m * feats),
            transcendentals=0,
        ),
        compiler_params=pltpu.CompilerParams(vmem_limit_bytes=4 * VMEM_LIMIT),
        name="base_product",
    )(core, weights, *pieces)


def parts_kernel(down_ref, up_ref, in_ref, cols_ref, out_ref):
    nblocks = down_ref.shape[0]
    block = in_ref.shape[0] // nblocks
    dims = (((1,), (1,)), ((), ()))
    for i, (factor, rows_ref) in enumerate(((down_ref, in_ref), (up_ref, cols_ref))):
        for b in range(nblocks):
            rows = rows_ref[b * block : (b + 1) * block, :]
            part = lax.dot_general(factor[b], rows, dims, preferred_element_type=F32)
            for to in range(out_ref.shape[0]):
                out_ref[to, i * nblocks + b] = part


def rank_parts(sel_down, sel_up, inputs, cols):
    nblocks, rank, _ = sel_down.shape
    vmem = pl.BlockSpec(memory_space=pltpu.VMEM)
    return pl.pallas_call(
        parts_kernel,
        out_shape=jax.ShapeDtypeStruct((X * CORE, 2 * nblocks, rank, inputs.shape[0] // nblocks), F32),
        in_specs=[vmem] * 4,
        out_specs=vmem,
        cost_estimate=pl.CostEstimate(flops=4 * rank * inputs.size, bytes_accessed=6 * inputs.size, transcendentals=0),
        compiler_params=pltpu.CompilerParams(vmem_limit_bytes=VMEM_LIMIT),
        name="rank_parts",
    )(sel_down, sel_up, inputs, cols)


def grads_kernel(ids_ref, own_ref, got_ref, in_ref, cols_ref, out_ref, proj_ref):
    nblocks = own_ref.shape[0] // 2
    block, wide = in_ref.shape[0] // nblocks, in_ref.shape[1]
    share = own_ref.shape[1] // DP
    proj = (own_ref[...] + got_ref[...]).astype(BF16)
    proj_ref[...] = proj[nblocks:]
    dims = (((1,), (0,)), ((), ()))
    for b in range(nblocks):
        rows = slice(b * block, (b + 1) * block)
        down = lax.dot_general(proj[nblocks + b], in_ref[rows, :], dims, preferred_element_type=F32)
        up = lax.dot_general(proj[b], cols_ref[rows, :], dims, preferred_element_type=F32)
        for i, grad in enumerate((SCALE * down, SCALE * up)):
            at = (i * nblocks + b) * share
            for to in range(DP):
                out_ref[to, at : at + share, :] = grad[to * share : (to + 1) * share]
    lane = lax.broadcasted_iota(jnp.int32, (1, wide), 1)
    ids = jnp.zeros((1, wide), F32)
    for b in range(nblocks):
        ids = jnp.where(lane == b, ids_ref[0, b].astype(F32), ids)
    for to in range(DP):
        out_ref[to, 2 * nblocks * share :, :] = ids


def block_grads(tenant_index, own, got, inputs, cols):
    count, rank, block = own.shape
    nblocks = count // 2
    wide = inputs.shape[1]
    vmem = pl.BlockSpec(memory_space=pltpu.VMEM)
    smem = pl.BlockSpec(memory_space=pltpu.SMEM)
    return pl.pallas_call(
        grads_kernel,
        out_shape=[
            jax.ShapeDtypeStruct((DP, 2 * nblocks * rank // DP + 1, wide), F32),
            jax.ShapeDtypeStruct((nblocks, rank, block), BF16),
        ],
        in_specs=[smem] + [vmem] * 4,
        out_specs=[vmem, vmem],
        cost_estimate=pl.CostEstimate(flops=4 * rank * inputs.size, bytes_accessed=6 * inputs.size, transcendentals=0),
        compiler_params=pltpu.CompilerParams(vmem_limit_bytes=VMEM_LIMIT),
        name="block_grads",
    )(tenant_index, own, got, inputs, cols)


def join_kernel(nblocks, where_ref, proj_ref, down_ref, *refs):
    *parts, out_ref, adapter_ref = refs
    dims = (((0,), (0,)), ((), ()))
    terms = [SCALE * lax.dot_general(proj_ref[b], down_ref[b], dims, preferred_element_type=F32) for b in range(nblocks)]
    adapter_ref[...] = jnp.concatenate(terms, axis=0).reshape(adapter_ref.shape)
    count = parts[0].shape[0]
    for c in range(CORE):
        got = parts[2 * c + 1]
        for p in range(count):
            adapter_ref[where_ref[1, c * count + p]] += got[p].astype(F32)
    for c in range(CORE):
        keep = parts[2 * c]
        for p in range(count):
            to = where_ref[0, c * count + p]
            out_ref[to] = (keep[p].astype(F32) + adapter_ref[to]).astype(BF16)


def join(where, proj_out, sel_down, parts):
    count, m, feats = parts[0].shape
    shape = (CORE * count, m, feats)
    vmem = pl.BlockSpec(memory_space=pltpu.VMEM)
    smem = pl.BlockSpec(memory_space=pltpu.SMEM)
    return pl.pallas_call(
        functools.partial(join_kernel, proj_out.shape[0]),
        out_shape=jax.ShapeDtypeStruct(shape, BF16),
        in_specs=[smem] + [vmem] * (2 + len(parts)),
        out_specs=vmem,
        scratch_shapes=[pltpu.VMEM(shape, F32)],
        cost_estimate=pl.CostEstimate(flops=0, bytes_accessed=20 * count * m * feats, transcendentals=0),
        compiler_params=pltpu.CompilerParams(vmem_limit_bytes=VMEM_LIMIT),
        name="join_rows",
    )(where, proj_out, sel_down, *parts)


def per_device(dy, inputs, weight, down, up, tenant_index, live_count):
    dy, inputs = dy[0], inputs[0]
    rows_here = dy.shape[0]
    nrows, in_width = inputs.shape
    nblocks = live_count.shape[1]
    block = nrows // nblocks
    tenants, rank, _ = down.shape
    zh, x, core = lax.axis_index("zh"), lax.axis_index("x"), lax.axis_index("core")
    kh, kl = lax.axis_index("kh"), lax.axis_index("kl")
    t = (zh * X + x) * CORE + core

    at = jnp.stack([t * rows_here, kh, kl]).astype(jnp.int32)
    same, other, cols = split_rows(dy, at, live_count, nblocks, block)

    swapped, _ = lax.optimization_barrier((lax.ppermute(weight, "kl", swap_pairs(KL, 1)), same))
    weights = lax.all_gather(turned(weight, swapped), ("dp", "core"), axis=0, tiled=False)
    weights = weights.reshape((DP, CORE, KL) + weight.shape[::-1])

    from_zh = lax.ppermute(same, "zh", swap_pairs(ZH, 1))
    from_both = lax.ppermute(other, ("zh", "kh"), swap_pairs(ZH * KH, 3))
    from_kh = lax.ppermute(other, "kh", swap_pairs(KH, 1))
    away, home = jnp.stack([from_kh, from_both]), jnp.stack([same, from_zh])
    hot = tenant_index[0][:, None] == lax.broadcasted_iota(jnp.int32, (nblocks, tenants), 1)
    hot = hot.astype(BF16)
    sel_down = jnp.einsum("bt,trd->brd", hot, down, preferred_element_type=F32).astype(BF16)
    sel_up = jnp.einsum("bt,trd->brd", hot, up, preferred_element_type=F32).astype(BF16)
    cols = exchange(cols, TENSOR)
    cols = cols.reshape(nrows, -1)
    parts = rank_parts(sel_down, sel_up, inputs, cols)
    parts = exchange(parts, ("x", "core"))
    away = jnp.broadcast_to(away[None], (X,) + away.shape)
    parts, away, home = lax.optimization_barrier((parts, away, home))
    parts = parts.sum(axis=0)
    parts_got = lax.ppermute(parts, "zh", swap_pairs(ZH, 1))

    parts_got, weights = lax.optimization_barrier((parts_got, weights))

    share = rank // DP
    grads, proj_out = block_grads(tenant_index, parts, parts_got, inputs, cols)

    away = exchange(away, "x")
    home = [lax.ppermute(home, "x", shift_pairs(X, offset)) if offset else home for offset in OFFSETS]
    away, grads = lax.optimization_barrier((away, grads))
    core_at = core[None].astype(jnp.int32)
    send, send_other = base_product(core_at, weights, [away], (BF16, BF16))
    sums = lax.ppermute(send, "kh", swap_pairs(KH, 1))
    sums_other = lax.ppermute(send_other, ("core", "kh"), swap_pairs(CORE * KH, 3))
    got = exchange(grads, "dp")
    home, send, got = lax.optimization_barrier((home, send, got))
    keep, keep_other = base_product(core_at, weights, home, (F32, BF16))
    keep_other = lax.ppermute(keep_other, "core", swap_pairs(CORE, 1))
    where = [
        [((zh + z) % ZH * X + at) * CORE + c for c in (core, 1 - core) for at in order for z in range(ZH)]
        for order in ([(x + X - offset) % X for offset in OFFSETS], range(X))
    ]
    where = jnp.stack([jnp.stack(row) for row in where]).astype(jnp.int32)

    ids = got[:, -1, :nblocks].astype(jnp.int32)
    got = got[:, :-1].reshape(DP, 2, nblocks, share, in_width)
    place = (ids[None] == lax.broadcasted_iota(jnp.int32, (tenants, DP, nblocks), 0)).astype(F32)
    out = jnp.einsum("tgb,gabsd->atsd", place, got, precision=lax.Precision.HIGHEST, preferred_element_type=F32)

    input_gradient = join(where, proj_out, sel_down, (keep, sums, keep_other, sums_other)).reshape(1, nrows, in_width)
    return input_gradient, out[0], out[1]


def solution(mesh):
    fine = Mesh(mesh.devices.reshape(ZH, X, CORE, DP, KH, KL), AXES)
    group = ("dp",) + TENANT
    return jax.shard_map(
        per_device,
        mesh=fine,
        in_specs=(
            P(group, TENSOR, None),
            P(group, None, TENSOR),
            P(TENSOR, group),
            P(TENANT, None, TENSOR),
            P(TENANT, None, TENSOR),
            P(group, None),
            P(group, None),
        ),
        out_specs=(P(group, None, TENSOR), P(TENANT, "dp", TENSOR), P(TENANT, "dp", TENSOR)),
        check_vma=False,
    )
```

```python
import functools

import jax
import jax.numpy as jnp
from jax import lax
from jax.experimental import pallas as pl
from jax.experimental.pallas import tpu as pltpu
from jax.sharding import Mesh, PartitionSpec as P

SCALE = 2.0
ZH, X, CORE, DP, KH, KL = 2, 4, 2, 8, 2, 2
TENSOR, TENANT = ("zh", "x", "core"), ("kh", "kl")
AXES = TENSOR + ("dp",) + TENANT
F32, BF16 = jnp.float32, jnp.bfloat16
OFFSETS = (0, 1, 3, 2)
VMEM_LIMIT = 12 * 2**20


def exchange(blocks, axes):
    return lax.all_to_all(blocks, axes, split_axis=0, concat_axis=0, tiled=True)


def swap_pairs(n, bit):
    return [(i, i ^ bit) for i in range(n)]


def shift_pairs(n, offset):
    return [(i, (i + offset) % n) for i in range(n)]


def split_kernel(nblocks, block, at_ref, live_ref, dy_ref, same_ref, other_ref, cols_ref):
    rows, width = dy_ref.shape
    first, kh, kl = at_ref[0], at_ref[1], at_ref[2]
    row = first + lax.broadcasted_iota(jnp.int32, (rows, 1), 0)
    live = jnp.zeros((rows, 1), jnp.int32)
    for b in range(nblocks):
        inside = (row >= b * block) & (row < b * block + live_ref[0, b])
        live = jnp.where(inside, 1, live)
    live = live > 0
    chunk = width // (DP * KH * KL)
    wide = cols_ref.shape[2]
    for d in range(DP):
        to = slice(d * chunk, (d + 1) * chunk)
        for low in range(KL):
            parts = []
            for h in range(KH):
                at = ((d * KH + h) * KL + low) * chunk
                part = jnp.where(live, dy_ref[:, at : at + chunk].astype(F32), 0.0)
                cols_ref[at // wide, :, at % wide : at % wide + chunk] = part.astype(BF16)
                parts.append(part)
            slot = lax.rem(kl + low, KL)
            same_ref[slot, :, to] = jnp.where(kh == 0, parts[0], parts[1]).astype(BF16)
            other_ref[slot, :, to] = jnp.where(kh == 0, parts[1], parts[0]).astype(BF16)


def split_rows(dy, at, live_count, nblocks, block):
    rows, width = dy.shape
    half = jax.ShapeDtypeStruct((KL, rows, width // (KH * KL)), BF16)
    shapes = [half, half, jax.ShapeDtypeStruct((ZH * X * CORE, rows, width // (ZH * X * CORE)), BF16)]
    vmem = pl.BlockSpec(memory_space=pltpu.VMEM)
    smem = pl.BlockSpec(memory_space=pltpu.SMEM)
    return pl.pallas_call(
        functools.partial(split_kernel, nblocks, block),
        out_shape=shapes,
        in_specs=[smem, smem, vmem],
        out_specs=[vmem] * len(shapes),
        cost_estimate=pl.CostEstimate(flops=0, bytes_accessed=3 * rows * width * 2, transcendentals=0),
        compiler_params=pltpu.CompilerParams(vmem_limit_bytes=VMEM_LIMIT),
        name="split_rows",
    )(at, live_count, dy)


def turn_kernel(from_ref, to_ref):
    to_ref[...] = from_ref[...].T


def pair_kernel(own_ref, got_ref, out_ref):
    out_ref[0] = own_ref[...]
    out_ref[1] = got_ref[...].T


def on_chip(kernel, name, shape, *operands):
    vmem = pl.BlockSpec(memory_space=pltpu.VMEM)
    return pl.pallas_call(
        kernel,
        out_shape=jax.ShapeDtypeStruct(shape, operands[0].dtype),
        in_specs=[vmem] * len(operands),
        out_specs=vmem,
        cost_estimate=pl.CostEstimate(flops=0, bytes_accessed=4 * sum(o.size for o in operands), transcendentals=0),
        compiler_params=pltpu.CompilerParams(vmem_limit_bytes=VMEM_LIMIT),
        name=name,
    )(*operands)


def base_kernel(core_ref, w_ref, *refs):
    pieces, outs, held_ref, sems = refs[: -CORE - 2], refs[-CORE - 2 : -2], refs[-2], refs[-1]
    copies = [pltpu.make_async_copy(w_ref.at[d], held_ref.at[d], sems.at[d]) for d in range(DP)]
    for copy in copies:
        copy.start()
    if len(pieces[0].shape) > 4:
        pieces = [pieces[0][i] for i in range(pieces[0].shape[0])]
    zs, _, m, depth = pieces[0].shape
    chunk = w_ref.shape[3]
    rows = [jnp.concatenate([piece[:, h].reshape(zs * m, depth) for piece in pieces], axis=0) for h in range(KL)]
    totals = [None] * CORE
    for d, copy in enumerate(copies):
        copy.wait()
        for i in range(CORE):
            at = lax.rem(core_ref[0] + i, CORE)
            for h in range(KL):
                term = lax.dot_general(
                    rows[h][:, d * chunk : (d + 1) * chunk], held_ref[d, at, h], (((1,), (0,)), ((), ())), preferred_element_type=F32
                )
                totals[i] = term if totals[i] is None else totals[i] + term
    for out, total in zip(outs, totals):
        out[...] = total.reshape(out.shape).astype(out.dtype)


def base_product(core, weights, pieces, dtypes):
    zs, _, m, _ = pieces[0].shape[-4:]
    count, feats = X * zs, weights.shape[4]
    vmem = pl.BlockSpec(memory_space=pltpu.VMEM)
    smem = pl.BlockSpec(memory_space=pltpu.SMEM)
    return pl.pallas_call(
        base_kernel,
        out_shape=[jax.ShapeDtypeStruct((count, m, feats), dtype) for dtype in dtypes],
        in_specs=[smem, pl.BlockSpec(memory_space=pl.ANY)] + [vmem] * len(pieces),
        out_specs=[vmem] * CORE,
        scratch_shapes=[pltpu.VMEM(weights.shape, weights.dtype), pltpu.SemaphoreType.DMA((DP,))],
        cost_estimate=pl.CostEstimate(
            flops=2 * count * m * weights.size,
            bytes_accessed=2 * (sum(p.size for p in pieces) + weights.size + 2 * count * m * feats),
            transcendentals=0,
        ),
        compiler_params=pltpu.CompilerParams(vmem_limit_bytes=4 * VMEM_LIMIT),
        name="base_product",
    )(core, weights, *pieces)


def parts_kernel(down_ref, up_ref, in_ref, cols_ref, out_ref):
    nblocks = down_ref.shape[0]
    block = in_ref.shape[0] // nblocks
    dims = (((1,), (1,)), ((), ()))
    for i, (factor, rows_ref) in enumerate(((down_ref, in_ref), (up_ref, cols_ref))):
        for b in range(nblocks):
            rows = rows_ref[b * block : (b + 1) * block, :]
            part = lax.dot_general(factor[b], rows, dims, preferred_element_type=F32)
            for to in range(out_ref.shape[0]):
                out_ref[to, i * nblocks + b] = part


def rank_parts(sel_down, sel_up, inputs, cols):
    nblocks, rank, _ = sel_down.shape
    vmem = pl.BlockSpec(memory_space=pltpu.VMEM)
    return pl.pallas_call(
        parts_kernel,
        out_shape=jax.ShapeDtypeStruct((X * CORE, 2 * nblocks, rank, inputs.shape[0] // nblocks), F32),
        in_specs=[vmem] * 4,
        out_specs=vmem,
        cost_estimate=pl.CostEstimate(flops=4 * rank * inputs.size, bytes_accessed=6 * inputs.size, transcendentals=0),
        compiler_params=pltpu.CompilerParams(vmem_limit_bytes=VMEM_LIMIT),
        name="rank_parts",
    )(sel_down, sel_up, inputs, cols)


def grads_kernel(ids_ref, own_ref, got_ref, in_ref, cols_ref, out_ref, proj_ref):
    nblocks = own_ref.shape[0] // 2
    block, wide = in_ref.shape[0] // nblocks, in_ref.shape[1]
    share = own_ref.shape[1] // DP
    proj = (own_ref[...] + got_ref[...]).astype(BF16)
    proj_ref[...] = proj[nblocks:]
    dims = (((1,), (0,)), ((), ()))
    for b in range(nblocks):
        rows = slice(b * block, (b + 1) * block)
        down = lax.dot_general(proj[nblocks + b], in_ref[rows, :], dims, preferred_element_type=F32)
        up = lax.dot_general(proj[b], cols_ref[rows, :], dims, preferred_element_type=F32)
        for i, grad in enumerate((SCALE * down, SCALE * up)):
            at = (i * nblocks + b) * share
            for to in range(DP):
                out_ref[to, at : at + share, :] = grad[to * share : (to + 1) * share]
    lane = lax.broadcasted_iota(jnp.int32, (1, wide), 1)
    ids = jnp.zeros((1, wide), F32)
    for b in range(nblocks):
        ids = jnp.where(lane == b, ids_ref[0, b].astype(F32), ids)
    for to in range(DP):
        out_ref[to, 2 * nblocks * share :, :] = ids


def block_grads(tenant_index, own, got, inputs, cols):
    count, rank, block = own.shape
    nblocks = count // 2
    wide = inputs.shape[1]
    vmem = pl.BlockSpec(memory_space=pltpu.VMEM)
    smem = pl.BlockSpec(memory_space=pltpu.SMEM)
    return pl.pallas_call(
        grads_kernel,
        out_shape=[
            jax.ShapeDtypeStruct((DP, 2 * nblocks * rank // DP + 1, wide), F32),
            jax.ShapeDtypeStruct((nblocks, rank, block), BF16),
        ],
        in_specs=[smem] + [vmem] * 4,
        out_specs=[vmem, vmem],
        cost_estimate=pl.CostEstimate(flops=4 * rank * inputs.size, bytes_accessed=6 * inputs.size, transcendentals=0),
        compiler_params=pltpu.CompilerParams(vmem_limit_bytes=VMEM_LIMIT),
        name="block_grads",
    )(tenant_index, own, got, inputs, cols)


def join_kernel(nblocks, where_ref, proj_ref, down_ref, *refs):
    *parts, out_ref, adapter_ref = refs
    dims = (((0,), (0,)), ((), ()))
    terms = [SCALE * lax.dot_general(proj_ref[b], down_ref[b], dims, preferred_element_type=F32) for b in range(nblocks)]
    adapter_ref[...] = jnp.concatenate(terms, axis=0).reshape(adapter_ref.shape)
    count = parts[0].shape[0]
    for c in range(CORE):
        got = parts[2 * c + 1]
        for p in range(count):
            adapter_ref[where_ref[1, c * count + p]] += got[p].astype(F32)
    for c in range(CORE):
        keep = parts[2 * c]
        for p in range(count):
            to = where_ref[0, c * count + p]
            out_ref[to] = (keep[p].astype(F32) + adapter_ref[to]).astype(BF16)


def join(where, proj_out, sel_down, parts):
    count, m, feats = parts[0].shape
    shape = (CORE * count, m, feats)
    vmem = pl.BlockSpec(memory_space=pltpu.VMEM)
    smem = pl.BlockSpec(memory_space=pltpu.SMEM)
    return pl.pallas_call(
        functools.partial(join_kernel, proj_out.shape[0]),
        out_shape=jax.ShapeDtypeStruct(shape, BF16),
        in_specs=[smem] + [vmem] * (2 + len(parts)),
        out_specs=vmem,
        scratch_shapes=[pltpu.VMEM(shape, F32)],
        cost_estimate=pl.CostEstimate(flops=0, bytes_accessed=20 * count * m * feats, transcendentals=0),
        compiler_params=pltpu.CompilerParams(vmem_limit_bytes=VMEM_LIMIT),
        name="join_rows",
    )(where, proj_out, sel_down, *parts)


def per_device(dy, inputs, weight, down, up, tenant_index, live_count):
    dy, inputs = dy[0], inputs[0]
    rows_here = dy.shape[0]
    nrows, in_width = inputs.shape
    nblocks = live_count.shape[1]
    block = nrows // nblocks
    tenants, rank, _ = down.shape
    zh, x, core = lax.axis_index("zh"), lax.axis_index("x"), lax.axis_index("core")
    kh, kl = lax.axis_index("kh"), lax.axis_index("kl")
    t = (zh * X + x) * CORE + core

    at = jnp.stack([t * rows_here, kh, kl]).astype(jnp.int32)
    same, other, cols = split_rows(dy, at, live_count, nblocks, block)

    swapped, _ = lax.optimization_barrier((lax.ppermute(weight, "kl", swap_pairs(KL, 1)), same))
    turned = on_chip(turn_kernel, "turned", weight.shape[::-1], weight)
    weights = on_chip(pair_kernel, "paired", (KL,) + turned.shape, turned, swapped)
    weights = lax.all_gather(weights, ("dp", "core"), axis=0, tiled=False)
    weights = weights.reshape((DP, CORE, KL) + weight.shape[::-1])

    from_zh = lax.ppermute(same, "zh", swap_pairs(ZH, 1))
    from_both = lax.ppermute(other, ("zh", "kh"), swap_pairs(ZH * KH, 3))
    from_kh = lax.ppermute(other, "kh", swap_pairs(KH, 1))
    away, home = jnp.stack([from_kh, from_both]), jnp.stack([same, from_zh])
    hot = tenant_index[0][:, None] == lax.broadcasted_iota(jnp.int32, (nblocks, tenants), 1)
    hot = hot.astype(BF16)
    sel_down = jnp.einsum("bt,trd->brd", hot, down, preferred_element_type=F32).astype(BF16)
    sel_up = jnp.einsum("bt,trd->brd", hot, up, preferred_element_type=F32).astype(BF16)
    cols = exchange(cols, TENSOR)
    cols = cols.reshape(nrows, -1)
    parts = rank_parts(sel_down, sel_up, inputs, cols)
    parts = exchange(parts, ("x", "core"))
    away = jnp.broadcast_to(away[None], (X,) + away.shape)
    parts, away, home = lax.optimization_barrier((parts, away, home))
    parts = parts.sum(axis=0)
    parts_got = lax.ppermute(parts, "zh", swap_pairs(ZH, 1))

    parts_got, weights = lax.optimization_barrier((parts_got, weights))

    share = rank // DP
    grads, proj_out = block_grads(tenant_index, parts, parts_got, inputs, cols)

    away = exchange(away, "x")
    home = [lax.ppermute(home, "x", shift_pairs(X, offset)) if offset else home for offset in OFFSETS]
    away, grads = lax.optimization_barrier((away, grads))
    core_at = core[None].astype(jnp.int32)
    send, send_other = base_product(core_at, weights, [away], (BF16, BF16))
    sums = lax.ppermute(send, "kh", swap_pairs(KH, 1))
    sums_other = lax.ppermute(send_other, ("core", "kh"), swap_pairs(CORE * KH, 3))
    got = exchange(grads, "dp")
    home, send, got = lax.optimization_barrier((home, send, got))
    keep, keep_other = base_product(core_at, weights, home, (F32, BF16))
    keep_other = lax.ppermute(keep_other, "core", swap_pairs(CORE, 1))
    where = [
        [((zh + z) % ZH * X + at) * CORE + c for c in (core, 1 - core) for at in order for z in range(ZH)]
        for order in ([(x + X - offset) % X for offset in OFFSETS], range(X))
    ]
    where = jnp.stack([jnp.stack(row) for row in where]).astype(jnp.int32)

    ids = got[:, -1, :nblocks].astype(jnp.int32)
    got = got[:, :-1].reshape(DP, 2, nblocks, share, in_width)
    place = (ids[None] == lax.broadcasted_iota(jnp.int32, (tenants, DP, nblocks), 0)).astype(F32)
    out = jnp.einsum("tgb,gabsd->atsd", place, got, precision=lax.Precision.HIGHEST, preferred_element_type=F32)

    input_gradient = join(where, proj_out, sel_down, (keep, sums, keep_other, sums_other)).reshape(1, nrows, in_width)
    return input_gradient, out[0], out[1]


def solution(mesh):
    fine = Mesh(mesh.devices.reshape(ZH, X, CORE, DP, KH, KL), AXES)
    group = ("dp",) + TENANT
    return jax.shard_map(
        per_device,
        mesh=fine,
        in_specs=(
            P(group, TENSOR, None),
            P(group, None, TENSOR),
            P(TENSOR, group),
            P(TENANT, None, TENSOR),
            P(TENANT, None, TENSOR),
            P(group, None),
            P(group, None),
        ),
        out_specs=(P(group, None, TENSOR), P(TENANT, "dp", TENSOR), P(TENANT, "dp", TENSOR)),
        check_vma=False,
    )
```

```python
import functools

import jax
import jax.numpy as jnp
from jax import lax
from jax.experimental import pallas as pl
from jax.experimental.pallas import tpu as pltpu
from jax.sharding import Mesh, PartitionSpec as P

SCALE = 2.0
ZH, X, CORE, DP, KH, KL = 2, 4, 2, 8, 2, 2
TENSOR, TENANT = ("zh", "x", "core"), ("kh", "kl")
AXES = TENSOR + ("dp",) + TENANT
F32, BF16 = jnp.float32, jnp.bfloat16
OFFSETS = (0, 1, 3, 2)
VMEM_LIMIT = 12 * 2**20


def exchange(blocks, axes):
    return lax.all_to_all(blocks, axes, split_axis=0, concat_axis=0, tiled=True)


def swap_pairs(n, bit):
    return [(i, i ^ bit) for i in range(n)]


def shift_pairs(n, offset):
    return [(i, (i + offset) % n) for i in range(n)]


def split_kernel(nblocks, block, at_ref, live_ref, dy_ref, same_ref, other_ref, cols_ref):
    rows, width = dy_ref.shape
    first, kh, kl = at_ref[0], at_ref[1], at_ref[2]
    row = first + lax.broadcasted_iota(jnp.int32, (rows, 1), 0)
    live = jnp.zeros((rows, 1), jnp.int32)
    for b in range(nblocks):
        inside = (row >= b * block) & (row < b * block + live_ref[0, b])
        live = jnp.where(inside, 1, live)
    live = live > 0
    chunk = width // (DP * KH * KL)
    wide = cols_ref.shape[2]
    for d in range(DP):
        to = slice(d * chunk, (d + 1) * chunk)
        for low in range(KL):
            parts = []
            for h in range(KH):
                at = ((d * KH + h) * KL + low) * chunk
                part = jnp.where(live, dy_ref[:, at : at + chunk].astype(F32), 0.0)
                cols_ref[at // wide, :, at % wide : at % wide + chunk] = part.astype(BF16)
                parts.append(part)
            slot = lax.rem(kl + low, KL)
            same_ref[slot, :, to] = jnp.where(kh == 0, parts[0], parts[1]).astype(BF16)
            other_ref[slot, :, to] = jnp.where(kh == 0, parts[1], parts[0]).astype(BF16)


def split_rows(dy, at, live_count, nblocks, block):
    rows, width = dy.shape
    half = jax.ShapeDtypeStruct((KL, rows, width // (KH * KL)), BF16)
    shapes = [half, half, jax.ShapeDtypeStruct((ZH * X * CORE, rows, width // (ZH * X * CORE)), BF16)]
    vmem = pl.BlockSpec(memory_space=pltpu.VMEM)
    smem = pl.BlockSpec(memory_space=pltpu.SMEM)
    return pl.pallas_call(
        functools.partial(split_kernel, nblocks, block),
        out_shape=shapes,
        in_specs=[smem, smem, vmem],
        out_specs=[vmem] * len(shapes),
        cost_estimate=pl.CostEstimate(flops=0, bytes_accessed=3 * rows * width * 2, transcendentals=0),
        compiler_params=pltpu.CompilerParams(vmem_limit_bytes=VMEM_LIMIT),
        name="split_rows",
    )(at, live_count, dy)


def turn_kernel(from_ref, to_ref):
    to_ref[...] = from_ref[...].T


def pair_kernel(own_ref, got_ref, out_ref):
    out_ref[0] = own_ref[...]
    out_ref[1] = got_ref[...].T


def on_chip(kernel, name, shape, *operands):
    vmem = pl.BlockSpec(memory_space=pltpu.VMEM)
    return pl.pallas_call(
        kernel,
        out_shape=jax.ShapeDtypeStruct(shape, operands[0].dtype),
        in_specs=[vmem] * len(operands),
        out_specs=vmem,
        cost_estimate=pl.CostEstimate(flops=0, bytes_accessed=4 * sum(o.size for o in operands), transcendentals=0),
        compiler_params=pltpu.CompilerParams(vmem_limit_bytes=VMEM_LIMIT),
        name=name,
    )(*operands)


def base_kernel(count, core_ref, w_ref, *refs):
    pieces, outs, held_ref, sems = refs[: -count - 2], refs[-count - 2 : -2], refs[-2], refs[-1]
    copies = [
        [pltpu.make_async_copy(w_ref.at[d, lax.rem(core_ref[0] + i, CORE)], held_ref.at[d, i], sems.at[d, i]) for i in range(count)]
        for d in range(DP)
    ]
    for pair in copies:
        for copy in pair:
            copy.start()
    if len(pieces[0].shape) > 4:
        pieces = [pieces[0][i] for i in range(pieces[0].shape[0])]
    zs, _, m, depth = pieces[0].shape
    chunk = w_ref.shape[3]
    rows = [jnp.concatenate([piece[:, h].reshape(zs * m, depth) for piece in pieces], axis=0) for h in range(KL)]
    totals = [None] * count
    for d, pair in enumerate(copies):
        for i, copy in enumerate(pair):
            copy.wait()
            for h in range(KL):
                term = lax.dot_general(
                    rows[h][:, d * chunk : (d + 1) * chunk], held_ref[d, i, h], (((1,), (0,)), ((), ())), preferred_element_type=F32
                )
                totals[i] = term if totals[i] is None else totals[i] + term
    for out, total in zip(outs, totals):
        out[...] = total.reshape(out.shape).astype(out.dtype)


def base_product(core, weights, pieces, dtypes):
    zs, _, m, _ = pieces[0].shape[-4:]
    rows, feats, count = X * zs, weights.shape[4], len(dtypes)
    vmem = pl.BlockSpec(memory_space=pltpu.VMEM)
    smem = pl.BlockSpec(memory_space=pltpu.SMEM)
    return pl.pallas_call(
        functools.partial(base_kernel, count),
        out_shape=[jax.ShapeDtypeStruct((rows, m, feats), dtype) for dtype in dtypes],
        in_specs=[smem, pl.BlockSpec(memory_space=pl.ANY)] + [vmem] * len(pieces),
        out_specs=[vmem] * count,
        scratch_shapes=[
            pltpu.VMEM((DP, count) + weights.shape[2:], weights.dtype),
            pltpu.SemaphoreType.DMA((DP, count)),
        ],
        cost_estimate=pl.CostEstimate(
            flops=count * rows * m * weights.size,
            bytes_accessed=2 * sum(p.size for p in pieces) + count * (weights.size + 2 * rows * m * feats),
            transcendentals=0,
        ),
        compiler_params=pltpu.CompilerParams(vmem_limit_bytes=4 * VMEM_LIMIT),
        name="base_product",
    )(core, weights, *pieces)


def parts_kernel(down_ref, up_ref, in_ref, cols_ref, out_ref):
    nblocks = down_ref.shape[0]
    block = in_ref.shape[0] // nblocks
    dims = (((1,), (1,)), ((), ()))
    for i, (factor, rows_ref) in enumerate(((down_ref, in_ref), (up_ref, cols_ref))):
        for b in range(nblocks):
            rows = rows_ref[b * block : (b + 1) * block, :]
            part = lax.dot_general(factor[b], rows, dims, preferred_element_type=F32)
            for to in range(out_ref.shape[0]):
                out_ref[to, i * nblocks + b] = part


def rank_parts(sel_down, sel_up, inputs, cols):
    nblocks, rank, _ = sel_down.shape
    vmem = pl.BlockSpec(memory_space=pltpu.VMEM)
    return pl.pallas_call(
        parts_kernel,
        out_shape=jax.ShapeDtypeStruct((X * CORE, 2 * nblocks, rank, inputs.shape[0] // nblocks), F32),
        in_specs=[vmem] * 4,
        out_specs=vmem,
        cost_estimate=pl.CostEstimate(flops=4 * rank * inputs.size, bytes_accessed=6 * inputs.size, transcendentals=0),
        compiler_params=pltpu.CompilerParams(vmem_limit_bytes=VMEM_LIMIT),
        name="rank_parts",
    )(sel_down, sel_up, inputs, cols)


def grads_kernel(ids_ref, own_ref, got_ref, in_ref, cols_ref, out_ref, proj_ref):
    nblocks = own_ref.shape[0] // 2
    block, wide = in_ref.shape[0] // nblocks, in_ref.shape[1]
    share = own_ref.shape[1] // DP
    proj = (own_ref[...] + got_ref[...]).astype(BF16)
    proj_ref[...] = proj[nblocks:]
    dims = (((1,), (0,)), ((), ()))
    for b in range(nblocks):
        rows = slice(b * block, (b + 1) * block)
        down = lax.dot_general(proj[nblocks + b], in_ref[rows, :], dims, preferred_element_type=F32)
        up = lax.dot_general(proj[b], cols_ref[rows, :], dims, preferred_element_type=F32)
        for i, grad in enumerate((SCALE * down, SCALE * up)):
            at = (i * nblocks + b) * share
            for to in range(DP):
                out_ref[to, at : at + share, :] = grad[to * share : (to + 1) * share]
    lane = lax.broadcasted_iota(jnp.int32, (1, wide), 1)
    ids = jnp.zeros((1, wide), F32)
    for b in range(nblocks):
        ids = jnp.where(lane == b, ids_ref[0, b].astype(F32), ids)
    for to in range(DP):
        out_ref[to, 2 * nblocks * share :, :] = ids


def block_grads(tenant_index, own, got, inputs, cols):
    count, rank, block = own.shape
    nblocks = count // 2
    wide = inputs.shape[1]
    vmem = pl.BlockSpec(memory_space=pltpu.VMEM)
    smem = pl.BlockSpec(memory_space=pltpu.SMEM)
    return pl.pallas_call(
        grads_kernel,
        out_shape=[
            jax.ShapeDtypeStruct((DP, 2 * nblocks * rank // DP + 1, wide), F32),
            jax.ShapeDtypeStruct((nblocks, rank, block), BF16),
        ],
        in_specs=[smem] + [vmem] * 4,
        out_specs=[vmem, vmem],
        cost_estimate=pl.CostEstimate(flops=4 * rank * inputs.size, bytes_accessed=6 * inputs.size, transcendentals=0),
        compiler_params=pltpu.CompilerParams(vmem_limit_bytes=VMEM_LIMIT),
        name="block_grads",
    )(tenant_index, own, got, inputs, cols)


def join_kernel(nblocks, where_ref, proj_ref, down_ref, *refs):
    *parts, out_ref, adapter_ref = refs
    dims = (((0,), (0,)), ((), ()))
    terms = [SCALE * lax.dot_general(proj_ref[b], down_ref[b], dims, preferred_element_type=F32) for b in range(nblocks)]
    adapter_ref[...] = jnp.concatenate(terms, axis=0).reshape(adapter_ref.shape)
    count = parts[0].shape[0]
    for c in range(CORE):
        got = parts[2 * c + 1]
        for p in range(count):
            adapter_ref[where_ref[1, c * count + p]] += got[p].astype(F32)
    for c in range(CORE):
        keep = parts[2 * c]
        for p in range(count):
            to = where_ref[0, c * count + p]
            out_ref[to] = (keep[p].astype(F32) + adapter_ref[to]).astype(BF16)


def join(where, proj_out, sel_down, parts):
    count, m, feats = parts[0].shape
    shape = (CORE * count, m, feats)
    vmem = pl.BlockSpec(memory_space=pltpu.VMEM)
    smem = pl.BlockSpec(memory_space=pltpu.SMEM)
    return pl.pallas_call(
        functools.partial(join_kernel, proj_out.shape[0]),
        out_shape=jax.ShapeDtypeStruct(shape, BF16),
        in_specs=[smem] + [vmem] * (2 + len(parts)),
        out_specs=vmem,
        scratch_shapes=[pltpu.VMEM(shape, F32)],
        cost_estimate=pl.CostEstimate(flops=0, bytes_accessed=20 * count * m * feats, transcendentals=0),
        compiler_params=pltpu.CompilerParams(vmem_limit_bytes=VMEM_LIMIT),
        name="join_rows",
    )(where, proj_out, sel_down, *parts)


def per_device(dy, inputs, weight, down, up, tenant_index, live_count):
    dy, inputs = dy[0], inputs[0]
    rows_here = dy.shape[0]
    nrows, in_width = inputs.shape
    nblocks = live_count.shape[1]
    block = nrows // nblocks
    tenants, rank, _ = down.shape
    zh, x, core = lax.axis_index("zh"), lax.axis_index("x"), lax.axis_index("core")
    kh, kl = lax.axis_index("kh"), lax.axis_index("kl")
    t = (zh * X + x) * CORE + core

    at = jnp.stack([t * rows_here, kh, kl]).astype(jnp.int32)
    same, other, cols = split_rows(dy, at, live_count, nblocks, block)

    swapped, _ = lax.optimization_barrier((lax.ppermute(weight, "kl", swap_pairs(KL, 1)), same))
    turned = on_chip(turn_kernel, "turned", weight.shape[::-1], weight)
    weights = on_chip(pair_kernel, "paired", (KL,) + turned.shape, turned, swapped)
    weights = lax.all_gather(weights, ("dp", "core"), axis=0, tiled=False)
    weights = weights.reshape((DP, CORE, KL) + weight.shape[::-1])

    from_zh = lax.ppermute(same, "zh", swap_pairs(ZH, 1))
    from_both = lax.ppermute(other, ("zh", "kh"), swap_pairs(ZH * KH, 3))
    from_kh = lax.ppermute(other, "kh", swap_pairs(KH, 1))
    away, home = jnp.stack([from_kh, from_both]), jnp.stack([same, from_zh])
    hot = tenant_index[0][:, None] == lax.broadcasted_iota(jnp.int32, (nblocks, tenants), 1)
    hot = hot.astype(BF16)
    sel_down = jnp.einsum("bt,trd->brd", hot, down, preferred_element_type=F32).astype(BF16)
    sel_up = jnp.einsum("bt,trd->brd", hot, up, preferred_element_type=F32).astype(BF16)
    cols = exchange(cols, TENSOR)
    cols = cols.reshape(nrows, -1)
    parts = rank_parts(sel_down, sel_up, inputs, cols)
    parts = exchange(parts, ("x", "core"))
    away = jnp.broadcast_to(away[None], (X,) + away.shape)
    parts, away, home = lax.optimization_barrier((parts, away, home))
    parts = parts.sum(axis=0)
    parts_got = lax.ppermute(parts, "zh", swap_pairs(ZH, 1))

    parts_got, weights = lax.optimization_barrier((parts_got, weights))

    share = rank // DP
    grads, proj_out = block_grads(tenant_index, parts, parts_got, inputs, cols)

    away = exchange(away, "x")
    home = [lax.ppermute(home, "x", shift_pairs(X, offset)) if offset else home for offset in OFFSETS]
    away, grads = lax.optimization_barrier((away, grads))
    core_at = core[None].astype(jnp.int32)
    other_at = 1 - core_at
    (send,) = base_product(core_at, weights, [away], (BF16,))
    sums = lax.ppermute(send, "kh", swap_pairs(KH, 1))
    (send_other,) = base_product(other_at, weights, [away], (BF16,))
    sums_other = lax.ppermute(send_other, ("core", "kh"), swap_pairs(CORE * KH, 3))
    got = exchange(grads, "dp")
    home, send_other, got = lax.optimization_barrier((home, send_other, got))
    keep, keep_other = base_product(core_at, weights, home, (F32, BF16))
    keep_other = lax.ppermute(keep_other, "core", swap_pairs(CORE, 1))
    where = [
        [((zh + z) % ZH * X + at) * CORE + c for c in (core, 1 - core) for at in order for z in range(ZH)]
        for order in ([(x + X - offset) % X for offset in OFFSETS], range(X))
    ]
    where = jnp.stack([jnp.stack(row) for row in where]).astype(jnp.int32)

    ids = got[:, -1, :nblocks].astype(jnp.int32)
    got = got[:, :-1].reshape(DP, 2, nblocks, share, in_width)
    place = (ids[None] == lax.broadcasted_iota(jnp.int32, (tenants, DP, nblocks), 0)).astype(F32)
    out = jnp.einsum("tgb,gabsd->atsd", place, got, precision=lax.Precision.HIGHEST, preferred_element_type=F32)

    input_gradient = join(where, proj_out, sel_down, (keep, sums, keep_other, sums_other)).reshape(1, nrows, in_width)
    return input_gradient, out[0], out[1]


def solution(mesh):
    fine = Mesh(mesh.devices.reshape(ZH, X, CORE, DP, KH, KL), AXES)
    group = ("dp",) + TENANT
    return jax.shard_map(
        per_device,
        mesh=fine,
        in_specs=(
            P(group, TENSOR, None),
            P(group, None, TENSOR),
            P(TENSOR, group),
            P(TENANT, None, TENSOR),
            P(TENANT, None, TENSOR),
            P(group, None),
            P(group, None),
        ),
        out_specs=(P(group, None, TENSOR), P(TENANT, "dp", TENSOR), P(TENANT, "dp", TENSOR)),
        check_vma=False,
    )
```
